32 devices in a mesh: parts: 2 (over y), dp: 8 (over z, x), tensor: 2 (over core).
Axes of the slice: x: 2, y: 2, z: 4, core: 2. Of those that a mesh axis runs over, the one named last changes fastest.
Arguments:
- features: bfloat16 [2048, 8192], P(('parts', 'dp'), 'tensor'), parts along dimension 0, may hold values from -6 to 6
- cotangent: bfloat16 [2048, 8192], P(('parts', 'dp'), 'tensor'), parts along dimension 0, may hold values from -6 to 6
- tenant_ids: int32 [2048], P(('parts', 'dp')), parts along dimension 0, may hold values from 0 to 7, as said below
- document_index_per_token: int32 [2048], P(('parts', 'dp')), parts along dimension 0, may hold values from 0 to 1023, as said below
- owner_map: int32 [8], replicated, may hold values from 0 to 7, each once
- adapter_down: bfloat16 [8, 32, 8192], P('dp', None, 'tensor'), may hold values from -0.25 to 0.25
- adapter_up: bfloat16 [8, 32, 8192], P('dp', None, 'tensor'), may hold values from -0.0625 to 0.0625
Outputs:
- input_grad: bfloat16 [2048, 8192], P(('parts', 'dp'), 'tensor'), parts along dimension 0
- grad_down: float32 [16, 32, 8192], P(('parts', 'dp'), None, 'tensor'), parts along dimension 0
- up_adapter_gradient: float32 [16, 32, 8192], P(('parts', 'dp'), None, 'tensor'), parts along dimension 0
The draws below stay inside these ranges and needn't reach their ends.
There are 2 independent parts, one for each index of `parts`. The reference program is written for one: setup_inputs(seed, part) draws one part's arguments, and reference() takes and returns one part's arrays. A program takes and returns all parts, laid end to end along the dimension named above; an argument that names none is the same for every part. Nothing has to cross between parts.
Inputs may be any that keep to these rules, and one draw needn't show every extreme that they name: `tenant_ids`: each tenant's tokens are contiguous within one device's 128 rows, and no tenant has more than 32 of them there; in every draw one tenant has exactly 32 tokens in every device's rows. `document_index_per_token`: never falling; a document's number is the position of its first token; each document lies within one device's rows and within one tenant's tokens; the last token is a document of its own.
All inputs are finite; a program needn't handle non-finite values.
Results may differ from the reference program's by a relative error of at most 0.005.
Values may be sent and summed in bfloat16 or wider, within the bound.
No kernel may reach another device: no remote copies, remote signals or barrier semaphores. Data moves between devices by JAX's collectives and lax.ppermute only.
A program may use at most 64 MiB of HBM per device.

```python
import jax
import jax.numpy as jnp
from jax import lax

D = 8192
R = 32
TOK_DEV = 128
TOKENS = 1024
TENANTS = 8
CAP = 32
N_DP = 8


def tenant_layout(key):
    blocks = TOKENS // TOK_DEV
    pairs = N_DP * CAP
    full = jax.random.randint(jax.random.fold_in(key, 11), (), 0, N_DP)
    keys = jax.random.split(jax.random.fold_in(key, 12), blocks)

    def one_block(block_key):
        scores = jax.random.permutation(block_key, pairs).astype(jnp.int32)
        tenant_of = jnp.arange(pairs, dtype=jnp.int32) // CAP
        scores = jnp.where(tenant_of == full, scores - pairs, scores)
        order = jnp.argsort(scores, stable=True)[:TOK_DEV].astype(jnp.int32)
        chosen = jnp.sort(order)
        return chosen // CAP
    return jax.vmap(one_block)(keys).reshape(-1).astype(jnp.int32)


def draw_tenant_ids(key, part):
    layout = tenant_layout(key)
    return layout


def draw_document_index_per_token(key, part):
    tenant_total = tenant_layout(key)
    key = jax.random.fold_in(key, 5)
    cut = jax.random.randint(key, (TOKENS,), 0, 4) == 0
    positions = jnp.arange(TOKENS, dtype=jnp.int32)
    previous = jnp.concatenate([jnp.full((1,), -1, jnp.int32), tenant_total[:-1]])
    starts = (positions % TOK_DEV == 0) | (tenant_total != previous) | cut | (positions == TOKENS - 1)
    first_of = jnp.where(starts, positions, jnp.zeros_like(positions)).astype(jnp.int32)
    return lax.cummax(first_of, axis=0).astype(jnp.int32)


def block_levels(key, extent, pieces, low, high):
    def one(axis_at, blocks):
        draws = jax.random.uniform(jax.random.fold_in(jax.random.fold_in(key, 6), axis_at), (blocks,), jnp.float32, low / len(pieces), high / len(pieces))
        return jnp.repeat(jnp.exp(draws), extent[axis_at] // blocks).reshape((-1,) + (1,) * (len(extent) - axis_at - 1))

    gain = one(*pieces[0])
    for cut in pieces[1:]:
        gain = gain * one(*cut)
    return gain


def centred(stream_key, dims, scale, reach, shards=(), kind=jnp.bfloat16):
    result = jax.random.normal(stream_key, dims, jnp.float32) * scale
    if len(shards) > 0:
        result = block_levels(stream_key, dims, shards, -0.22, 0.18) * result
    return jnp.clip(result, min=-reach, max=reach).astype(kind)


def setup_inputs(seed: int = 0, part: int = 0) -> dict:
    splits = jax.random.split(jax.random.key(seed), 8)
    own_keys = jax.random.split(jax.random.fold_in(splits[7], part), 8)
    features = centred(own_keys[0], (TOKENS, D), 1.0, 6.0, ((0, 8), (1, 2)))
    cotangent = centred(own_keys[1], (TOKENS, D), 1.0, 6.0, ((0, 8), (1, 2)))
    tenant_ids = draw_tenant_ids(jax.random.fold_in(jax.random.fold_in(splits[7], part), 71), part)
    document_index_per_token = draw_document_index_per_token(jax.random.fold_in(jax.random.fold_in(splits[7], part), 71), part)
    owner_map = jax.random.permutation(splits[4], TENANTS).astype(jnp.int32)
    adapter_down = centred(splits[5], (N_DP, R, D), (16 * R) ** -0.5, 0.25, ((0, 8), (2, 2)))
    adapter_up = centred(splits[6], (N_DP, R, D), D ** -0.5, 0.0625, ((0, 8), (2, 2)))
    return dict(features=features, cotangent=cotangent, tenant_ids=tenant_ids, document_index_per_token=document_index_per_token, owner_map=owner_map, adapter_down=adapter_down, adapter_up=adapter_up)


adapter_scale_factor = 2.0


def reference(features, cotangent, tenant_ids, document_index_per_token, owner_map, adapter_down, adapter_up):
    slots = N_DP * CAP
    owner = owner_map[tenant_ids].astype(jnp.int32)
    token_count_per_tenant = jax.ops.segment_sum(jnp.ones((TOKENS,), jnp.float32), document_index_per_token, num_segments=TOKENS)
    routing_weight = adapter_scale_factor / token_count_per_tenant[document_index_per_token]

    def per_owner(rank):
        mine = owner == rank
        count = jnp.sum(mine.astype(jnp.int32))
        index = jnp.nonzero(mine, size=slots, fill_value=0)[0].astype(jnp.int32)
        valid = jnp.arange(slots, dtype=jnp.int32) < count
        rows_x = features[index]
        rows_g = cotangent[index]
        slot_weight = jnp.where(valid, routing_weight[index], jnp.zeros_like(routing_weight[index]))
        down = adapter_down[rank]
        up = adapter_up[rank]
        low_h = jnp.dot(rows_x, down.T, preferred_element_type=jnp.float32)
        low_u = jnp.dot(rows_g, up.T, preferred_element_type=jnp.float32)
        scaled_h = (low_h * slot_weight[:, None]).astype(jnp.bfloat16)
        scaled_u = (low_u * slot_weight[:, None]).astype(jnp.bfloat16)
        up_adapter_gradient = jnp.dot(scaled_h.T, rows_g, preferred_element_type=jnp.float32)
        grad_down = jnp.dot(scaled_u.T, rows_x, preferred_element_type=jnp.float32)
        slot_dx = jnp.dot(scaled_u, down, preferred_element_type=jnp.float32).astype(jnp.bfloat16)
        target = jnp.where(valid, index, jnp.int32(TOKENS)).astype(jnp.int32)
        return slot_dx, target, grad_down, up_adapter_gradient

    slot_dx, target, grad_down, up_adapter_gradient = lax.map(per_owner, jnp.arange(N_DP, dtype=jnp.int32))
    input_grad = jnp.zeros((TOKENS, D), jnp.bfloat16).at[target.reshape(-1)].set(slot_dx.reshape(-1, D), mode="drop")
    return input_grad, grad_down, up_adapter_gradient
```

```python
import jax
import jax.numpy as jnp
from jax import lax
from jax.sharding import PartitionSpec as P

adapter_scale_factor = 2.0


def contract_last(left, right):
    return lax.dot_general(
        left, right, (((1,), (1,)), ((), ())), preferred_element_type=jnp.float32
    )


def contract_first(left, right):
    return lax.dot_general(
        left, right, (((0,), (0,)), ((), ())), preferred_element_type=jnp.float32
    )


def token_owner(tenant_ids, owner_map):
    tenant_total = owner_map.shape[0]
    match = tenant_ids[:, None] == jnp.arange(tenant_total, dtype=jnp.int32)[None, :]
    return jnp.sum(jnp.where(match, owner_map[None, :], 0), axis=1)


def token_weight(document_index_per_token):
    same_doc = document_index_per_token[:, None] == document_index_per_token[None, :]
    sequence_length = jnp.sum(same_doc.astype(jnp.float32), axis=1)
    return adapter_scale_factor / sequence_length


def route_tokens(
    features, cotangent, tenant_ids, document_index_per_token, owner_map, adapter_down, adapter_up
):
    ranks = lax.axis_size("dp")
    rows = features.shape[0]
    width = features.shape[1]
    capacity = max(2, 2 * rows // ranks)
    slots = ranks * capacity
    token_row_index = jnp.arange(rows, dtype=jnp.int32)
    target = token_owner(tenant_ids, owner_map)
    routing_weight = token_weight(document_index_per_token)
    earlier = (token_row_index[:, None] > token_row_index[None, :]) & (
        target[:, None] == target[None, :]
    )
    before = jnp.sum(earlier.astype(jnp.int32), axis=1)
    slot_of = target * capacity + before
    placed = slot_of[None, :] == jnp.arange(slots, dtype=jnp.int32)[:, None]
    slot_weight = jnp.sum(
        jnp.where(placed, routing_weight[None, :], jnp.zeros_like(routing_weight)[None, :]), axis=1
    )

    def pack(values):
        return jnp.dot(
            placed.astype(values.dtype), values, preferred_element_type=jnp.float32
        ).astype(values.dtype)

    def exchange(values):
        return lax.all_to_all(values, "dp", split_axis=0, concat_axis=0, tiled=True)

    down_own = adapter_down[0]
    up_own = adapter_up[0]
    got_x = exchange(pack(features).reshape(ranks, capacity, width)).reshape(slots, width)
    got_g = exchange(pack(cotangent).reshape(ranks, capacity, width)).reshape(slots, width)
    got_w = exchange(slot_weight.reshape(ranks, capacity)).reshape(slots)
    low_h, low_u = lax.psum(
        (contract_last(got_x, down_own), contract_last(got_g, up_own)), "tensor"
    )
    scaled_h = (low_h * got_w[:, None]).astype(jnp.bfloat16)
    scaled_u = (low_u * got_w[:, None]).astype(jnp.bfloat16)
    up_adapter_gradient = contract_first(scaled_h, got_g)
    grad_down = contract_first(scaled_u, got_x)
    slot_dx = jnp.dot(scaled_u, down_own, preferred_element_type=jnp.float32).astype(jnp.bfloat16)
    returned = exchange(slot_dx.reshape(ranks, capacity, width)).reshape(slots, width)
    input_grad = contract_first(placed.astype(jnp.bfloat16), returned).astype(jnp.bfloat16)
    return (input_grad, grad_down[None], up_adapter_gradient[None])


def route_adapters(
    features, cotangent, tenant_ids, document_index_per_token, owner_map, adapter_down, adapter_up
):
    ranks = lax.axis_size("dp")
    columns = ranks // 2
    rows, width = features.shape
    rank = adapter_down.shape[1]
    half = rank // 2
    me = lax.axis_index("dp")
    side, place = me % 2, me // 2
    layer = lax.axis_index("parts")

    def swap_side(value):
        return lax.ppermute(value, "dp", [(i, i ^ 1) for i in range(ranks)])

    def shift(value, by):
        return lax.ppermute(value, "dp", [(i, (i + 2 * by) % ranks) for i in range(ranks)])

    def swap_layer(value):
        return lax.ppermute(value, "parts", [(0, 1), (1, 0)])

    def swap_core(value):
        return lax.ppermute(value, "tensor", [(0, 1), (1, 0)])

    def column_adapters(own):
        mine = lax.dynamic_slice(own, (layer * half, 0), (half, width))
        blocks = [own]
        for step in range(1, columns):
            got = shift(mine, -step)
            other = swap_layer(got)
            blocks.append(
                jnp.where(
                    layer == 0, jnp.concatenate([got, other]), jnp.concatenate([other, got])
                )
            )
        return jnp.concatenate(blocks)

    owner = token_owner(tenant_ids, owner_map)
    weight = token_weight(document_index_per_token)
    facts = jnp.stack([owner.astype(jnp.float32), weight])
    facts = jnp.concatenate([facts, swap_side(facts)], axis=1)
    owner_here = facts[0].astype(jnp.int32)
    weight_here = facts[1]
    steps = jnp.arange(columns, dtype=jnp.int32)
    block_owner = ((place + steps) % columns) * 2 + side
    block_owner_there = block_owner + 1 - 2 * side
    held = (block_owner[:, None] == owner_here[None, :])[:, None, :]
    own_held = (block_owner[:, None] == owner[None, :])[:, None, :]
    own_there = (block_owner_there[:, None] == owner[None, :])[:, None, :]

    def spread(low, mask):
        return jnp.where(mask, low[None], jnp.zeros((), low.dtype)).reshape(
            mask.shape[0] * rank, low.shape[1]
        )

    def project(adapters, own_rows, other_rows):
        low = jnp.concatenate(
            [contract_last(adapters, own_rows), contract_last(adapters, other_rows)], axis=1
        ).reshape(columns, rank, 2 * rows)
        low = jnp.sum(jnp.where(held, low, 0.0), axis=0)
        low = low + swap_core(low)
        return (low * weight_here[None, :]).astype(jnp.bfloat16)

    def gradient(scaled, own_rows, other_rows, pieces):
        left = spread(scaled, held)
        wide = width // pieces
        parts = []
        for piece in range(pieces):
            cut = slice(piece * wide, (piece + 1) * wide)
            total = jnp.dot(
                left[:, :rows], own_rows[:, cut], preferred_element_type=jnp.float32
            ) + jnp.dot(left[:, rows:], other_rows[piece], preferred_element_type=jnp.float32)
            sum_own = total[:rank]
            for step in range(1, columns):
                block = total[step * rank : (step + 1) * rank].astype(jnp.bfloat16)
                sum_own = sum_own + shift(block, step).astype(jnp.float32)
            parts.append(sum_own)
        return jnp.concatenate(parts, axis=1)

    pieces = 2
    wide = width // pieces
    other_x = [swap_side(features[:, i * wide : (i + 1) * wide]) for i in range(pieces)]
    down = column_adapters(adapter_down[0])
    up = column_adapters(adapter_up[0])
    other_g = [swap_side(cotangent[:, i * wide : (i + 1) * wide]) for i in range(pieces)]
    scaled_h = project(down, features, jnp.concatenate(other_x, axis=1))
    up_adapter_gradient = gradient(scaled_h, cotangent, other_g, pieces)
    scaled_u = project(up, cotangent, jnp.concatenate(other_g, axis=1))
    grad_down = gradient(scaled_u, features, other_x, pieces)
    down_there = swap_side(down)
    back = swap_side(scaled_u[:, rows:])
    left = jnp.concatenate([spread(scaled_u[:, :rows], own_held), spread(back, own_there)])
    input_grad = contract_first(left, jnp.concatenate([down, down_there])).astype(jnp.bfloat16)
    return (input_grad, grad_down[None], up_adapter_gradient[None])


def shards(features, *others):
    ranks = lax.axis_size("dp")
    rank = others[-1].shape[1]
    slots = 2 * features.shape[0] // ranks
    if slots >= rank and ranks % 2 == 0 and rank % 32 == 0 and lax.axis_size("parts") == 2:
        return route_adapters(features, *others)
    return route_tokens(features, *others)


def solution(mesh):
    return jax.shard_map(
        shards,
        mesh=mesh,
        in_specs=(
            P(("parts", "dp"), "tensor"),
            P(("parts", "dp"), "tensor"),
            P(("parts", "dp")),
            P(("parts", "dp")),
            P(),
            P("dp", None, "tensor"),
            P("dp", None, "tensor"),
        ),
        out_specs=(
            P(("parts", "dp"), "tensor"),
            P(("parts", "dp"), None, "tensor"),
            P(("parts", "dp"), None, "tensor"),
        ),
        check_vma=False,
    )
```

```python
import jax
import jax.numpy as jnp
from jax import lax
from jax.experimental import pallas as pl
from jax.experimental.pallas import tpu as pltpu
from jax.sharding import PartitionSpec as P

adapter_scale_factor = 2.0


def contract_last(left, right):
    return lax.dot_general(
        left, right, (((1,), (1,)), ((), ())), preferred_element_type=jnp.float32
    )


def contract_first(left, right):
    return lax.dot_general(
        left, right, (((0,), (0,)), ((), ())), preferred_element_type=jnp.float32
    )


def token_owner(tenant_ids, owner_map):
    tenant_total = owner_map.shape[0]
    match = tenant_ids[:, None] == jnp.arange(tenant_total, dtype=jnp.int32)[None, :]
    return jnp.sum(jnp.where(match, owner_map[None, :], 0), axis=1)


def token_weight(document_index_per_token):
    same_doc = document_index_per_token[:, None] == document_index_per_token[None, :]
    sequence_length = jnp.sum(same_doc.astype(jnp.float32), axis=1)
    return adapter_scale_factor / sequence_length


def after(value, *others):
    return lax.optimization_barrier((value,) + others)[0]


def route_tokens(
    features, cotangent, tenant_ids, document_index_per_token, owner_map, adapter_down, adapter_up
):
    ranks = lax.axis_size("dp")
    rows = features.shape[0]
    width = features.shape[1]
    capacity = max(2, 2 * rows // ranks)
    slots = ranks * capacity
    token_row_index = jnp.arange(rows, dtype=jnp.int32)
    target = token_owner(tenant_ids, owner_map)
    routing_weight = token_weight(document_index_per_token)
    earlier = (token_row_index[:, None] > token_row_index[None, :]) & (
        target[:, None] == target[None, :]
    )
    before = jnp.sum(earlier.astype(jnp.int32), axis=1)
    slot_of = target * capacity + before
    placed = slot_of[None, :] == jnp.arange(slots, dtype=jnp.int32)[:, None]
    slot_weight = jnp.sum(
        jnp.where(placed, routing_weight[None, :], jnp.zeros_like(routing_weight)[None, :]), axis=1
    )

    def pack(values):
        return jnp.dot(
            placed.astype(values.dtype), values, preferred_element_type=jnp.float32
        ).astype(values.dtype)

    def exchange(values):
        return lax.all_to_all(values, "dp", split_axis=0, concat_axis=0, tiled=True)

    down_own = adapter_down[0]
    up_own = adapter_up[0]
    got_x = exchange(pack(features).reshape(ranks, capacity, width)).reshape(slots, width)
    got_g = exchange(pack(cotangent).reshape(ranks, capacity, width)).reshape(slots, width)
    got_w = exchange(slot_weight.reshape(ranks, capacity)).reshape(slots)
    low_h, low_u = lax.psum(
        (contract_last(got_x, down_own), contract_last(got_g, up_own)), "tensor"
    )
    scaled_h = (low_h * got_w[:, None]).astype(jnp.bfloat16)
    scaled_u = (low_u * got_w[:, None]).astype(jnp.bfloat16)
    up_adapter_gradient = contract_first(scaled_h, got_g)
    grad_down = contract_first(scaled_u, got_x)
    slot_dx = jnp.dot(scaled_u, down_own, preferred_element_type=jnp.float32).astype(jnp.bfloat16)
    returned = exchange(slot_dx.reshape(ranks, capacity, width)).reshape(slots, width)
    input_grad = contract_first(placed.astype(jnp.bfloat16), returned).astype(jnp.bfloat16)
    return (input_grad, grad_down[None], up_adapter_gradient[None])


VMEM_LIMIT = 32 * 1024 * 1024


def whole(*shape):
    return pl.BlockSpec(shape, lambda _: (0,) * len(shape))


def column_cut(rows, wide, at):
    return pl.BlockSpec((rows, wide), lambda _: (0, at))


def cost(flops, moved):
    return pl.CostEstimate(flops=flops, bytes_accessed=moved, transcendentals=0)


def join_kernel(layer_ref, own_ref, *refs):
    *halves, out_ref = refs
    count = len(halves) // 2
    rank = own_ref.shape[0]
    out_ref[:rank, :] = own_ref[...]
    first = layer_ref[0] == 0
    for step in range(count):
        got, other = halves[step][...], halves[count + step][...]
        low = (step + 1) * rank
        middle = low + rank // 2
        out_ref[low:middle, :] = jnp.where(first, got, other)
        out_ref[middle : low + rank, :] = jnp.where(first, other, got)


def join(layer, own, got, other):
    rank, width = own.shape
    rows = (len(got) + 1) * rank
    return pl.pallas_call(
        join_kernel,
        grid=(1,),
        out_shape=jax.ShapeDtypeStruct((rows, width), own.dtype),
        in_specs=[pl.BlockSpec(memory_space=pltpu.SMEM), whole(rank, width)]
        + [whole(rank // 2, width)] * (2 * len(got)),
        out_specs=whole(rows, width),
        compiler_params=pltpu.CompilerParams(vmem_limit_bytes=VMEM_LIMIT),
        cost_estimate=cost(0, 4 * rows * width),
    )(layer, own, *got, *other)


def project_kernel(adapter_ref, own_ref, other_ref, held_ref, base_ref, out_ref):
    columns, tokens = held_ref.shape
    rows = tokens // 2
    rank = adapter_ref.shape[0] // columns
    adapters = adapter_ref[...]
    for part, rows_ref in enumerate((own_ref, other_ref)):
        cut = slice(part * rows, (part + 1) * rows)
        low = contract_last(adapters, rows_ref[...])
        total = base_ref[:, cut]
        for step in range(columns):
            total = total + jnp.where(
                held_ref[step : step + 1, cut] > 0, low[step * rank : (step + 1) * rank], 0.0
            )
        out_ref[:, cut] = total


def project(adapters, own_rows, other_rows, held, base, at):
    rows, wide = other_rows.shape
    height = adapters.shape[0]
    return pl.pallas_call(
        project_kernel,
        grid=(1,),
        out_shape=jax.ShapeDtypeStruct(base.shape, jnp.float32),
        in_specs=[
            column_cut(height, wide, at),
            column_cut(rows, wide, at),
            whole(rows, wide),
            whole(*held.shape),
            whole(*base.shape),
        ],
        out_specs=whole(*base.shape),
        compiler_params=pltpu.CompilerParams(vmem_limit_bytes=VMEM_LIMIT),
        cost_estimate=cost(4 * height * rows * wide, 2 * wide * (height + 2 * rows)),
    )(adapters, own_rows, other_rows, held, base)


def partial_kernel(scaled_ref, held_ref, own_ref, other_ref, sum_ref, *send_refs):
    columns, tokens = held_ref.shape
    rows = tokens // 2
    rank = scaled_ref.shape[0]
    scaled = scaled_ref[...]
    left = jnp.concatenate(
        [
            jnp.where(held_ref[step : step + 1, :] > 0, scaled, 0.0).astype(jnp.bfloat16)
            for step in range(columns)
        ]
    )
    total = jnp.dot(left[:, :rows], own_ref[...], preferred_element_type=jnp.float32)
    total = total + jnp.dot(left[:, rows:], other_ref[...], preferred_element_type=jnp.float32)
    sum_ref[...] = total[:rank]
    for step, send_ref in enumerate(send_refs):
        send_ref[...] = total[(step + 1) * rank : (step + 2) * rank].astype(jnp.bfloat16)


def partials(scaled, held, own_rows, other_rows, at):
    columns, tokens = held.shape
    rows, wide = other_rows.shape
    rank = scaled.shape[0]
    return pl.pallas_call(
        partial_kernel,
        grid=(1,),
        out_shape=[jax.ShapeDtypeStruct((rank, wide), jnp.float32)]
        + [jax.ShapeDtypeStruct((rank, wide), jnp.bfloat16)] * (columns - 1),
        in_specs=[
            whole(*scaled.shape),
            whole(*held.shape),
            column_cut(rows, wide, at),
            whole(rows, wide),
        ],
        out_specs=[whole(rank, wide)] * columns,
        compiler_params=pltpu.CompilerParams(vmem_limit_bytes=VMEM_LIMIT),
        cost_estimate=cost(2 * columns * rank * tokens * wide, 8 * rows * wide),
    )(scaled, held, own_rows, other_rows)


def route_adapters(
    features, cotangent, tenant_ids, document_index_per_token, owner_map, adapter_down, adapter_up
):
    ranks = lax.axis_size("dp")
    columns = ranks // 2
    rows, width = features.shape
    rank = adapter_down.shape[1]
    half = rank // 2
    me = lax.axis_index("dp")
    side, place = me % 2, me // 2
    layer = lax.axis_index("parts")

    def swap_side(value):
        return lax.ppermute(value, "dp", [(i, i ^ 1) for i in range(ranks)])

    def shift(value, by):
        return lax.ppermute(value, "dp", [(i, (i + 2 * by) % ranks) for i in range(ranks)])

    def swap_layer(value):
        return lax.ppermute(value, "parts", [(0, 1), (1, 0)])

    def swap_core(value):
        return lax.ppermute(value, "tensor", [(0, 1), (1, 0)])

    def half_rows(own):
        return lax.dynamic_slice(own, (layer * half, 0), (half, width))

    def fetch(own):
        return [shift(half_rows(own), -step) for step in range(1, columns)]

    def send(blocks):
        return [shift(block, step) for step, block in enumerate(blocks, 1)]

    def add(total, got):
        for block in got:
            total = total + block.astype(jnp.float32)
        return total

    pieces = 4
    wide = width // pieces
    layer_of = layer.astype(jnp.int32)[None]
    other_x = swap_side(features)
    down_got = fetch(adapter_down[0])
    down_other = [swap_layer(got) for got in down_got]
    up_own, cotangent, tenant_ids, document_index_per_token = lax.optimization_barrier(
        (adapter_up[0], cotangent, tenant_ids, document_index_per_token) + tuple(down_got)
    )[:4]
    other_g = [swap_side(cotangent[:, i * wide : (i + 1) * wide]) for i in range(pieces)]
    up_got = fetch(up_own)
    down = join(layer_of, adapter_down[0], down_got, down_other)

    owner = token_owner(tenant_ids, owner_map)
    weight = token_weight(document_index_per_token)
    facts = jnp.stack([owner.astype(jnp.float32), weight])
    facts = jnp.concatenate([facts, swap_side(after(facts, down))], axis=1)
    owner_here = facts[0].astype(jnp.int32)
    weight_here = facts[1]
    steps = jnp.arange(columns, dtype=jnp.int32)
    block_owner = ((place + steps) % columns) * 2 + side
    block_owner_there = block_owner + 1 - 2 * side
    held = (block_owner[:, None] == owner_here[None, :]).astype(jnp.float32)
    own_held = (block_owner[:, None] == owner[None, :])[:, None, :]
    own_there = (block_owner_there[:, None] == owner[None, :])[:, None, :]

    def spread(low, mask):
        return jnp.where(mask, low[None], jnp.zeros((), low.dtype)).reshape(
            columns * rank, low.shape[1]
        )

    def combine(low):
        return ((low + swap_core(low)) * weight_here[None, :]).astype(jnp.bfloat16)

    nothing = jnp.zeros((rank, 2 * rows), jnp.float32)
    low_h = project(down, features, other_x, held, nothing, 0)
    up_got = [after(got, low_h) for got in up_got]
    up = join(layer_of, up_own, up_got, [swap_layer(got) for got in up_got])
    scaled_h = combine(low_h)
    low_u = nothing
    totals, gots = [], []
    for i in range(pieces):
        if i > 1:
            other_g[i] = after(other_g[i], *gots[i - 2])
        total, *blocks = partials(scaled_h, held, cotangent, other_g[i], i)
        other_g[i] = after(other_g[i], total)
        totals.append(total)
        gots.append(send(blocks))
        low_u = project(up, cotangent, other_g[i], held, low_u, i)
    low_u = after(low_u, *gots[pieces - 2])
    scaled_u = combine(low_u)
    total, *blocks = partials(scaled_u, held, features, other_x, 0)
    got = send(blocks)
    back = swap_side(after(scaled_u, total)[:, rows:])
    down_there = swap_side(after(down, other_g[1]))
    up_adapter_gradient = jnp.concatenate([add(*pair) for pair in zip(totals, gots)], axis=1)
    left = jnp.concatenate([spread(scaled_u[:, :rows], own_held), spread(back, own_there)])
    input_grad = contract_first(left, jnp.concatenate([down, down_there])).astype(jnp.bfloat16)
    grad_down = add(total, got)
    return (input_grad, grad_down[None], up_adapter_gradient[None])


def shards(features, *others):
    ranks = lax.axis_size("dp")
    rank = others[-1].shape[1]
    slots = 2 * features.shape[0] // ranks
    if slots >= rank and ranks % 2 == 0 and rank % 32 == 0 and lax.axis_size("parts") == 2:
        return route_adapters(features, *others)
    return route_tokens(features, *others)


def solution(mesh):
    return jax.shard_map(
        shards,
        mesh=mesh,
        in_specs=(
            P(("parts", "dp"), "tensor"),
            P(("parts", "dp"), "tensor"),
            P(("parts", "dp")),
            P(("parts", "dp")),
            P(),
            P("dp", None, "tensor"),
            P("dp", None, "tensor"),
        ),
        out_specs=(
            P(("parts", "dp"), "tensor"),
            P(("parts", "dp"), None, "tensor"),
            P(("parts", "dp"), None, "tensor"),
        ),
        check_vma=False,
    )
```

```python
import functools

import jax
import jax.numpy as jnp
from jax import lax
from jax.experimental import pallas as pl
from jax.experimental.pallas import tpu as pltpu
from jax.sharding import PartitionSpec as P

adapter_scale_factor = 2.0
CFG = {'zero': True, 'cuts': ((0, 4), (4, 4)), 'xcuts': ((0, 4), (4, 4)), 'db': 'dd', 'da': 'split', 'fetch': 'half', 'ya': 'y3', 'yb': 'y3', 'zorder': (3, 2, 1), 'sorder': (1, 2, 3), 'a_ids_first': True, 'a_y2': False, 'a_y3y1': True, 'a_y3x': False, 'a_slice': False, 'a_up': 'z', 'a_upy': True, 'a_idsdown': True, 'a_g': False, 'a_xup': True, 'a_xg': 1, 'a_g0up': 1, 'a_prev': False, 'a_prev2': False, 'a_pu': True, 'a_last': 1, 'a_back': 'late', 'a_su': True, 'late_b': 0, 'a_there': None, 'a_chain': 0, 'a_backgot': 0, 'a_bz': False, 's2': (0, 2, 2, 2), 'fin': 'three'}


def contract_last(left, right):
    return lax.dot_general(
        left, right, (((1,), (1,)), ((), ())), preferred_element_type=jnp.float32
    )


def contract_first(left, right):
    return lax.dot_general(
        left, right, (((0,), (0,)), ((), ())), preferred_element_type=jnp.float32
    )


def token_owner(tenant_ids, owner_map):
    tenant_total = owner_map.shape[0]
    match = tenant_ids[:, None] == jnp.arange(tenant_total, dtype=jnp.int32)[None, :]
    return jnp.sum(jnp.where(match, owner_map[None, :], 0), axis=1)


def token_weight(document_index_per_token):
    same_doc = document_index_per_token[:, None] == document_index_per_token[None, :]
    sequence_length = jnp.sum(same_doc.astype(jnp.float32), axis=1)
    return adapter_scale_factor / sequence_length


def after(value, *others):
    return lax.optimization_barrier((value,) + others)[0]


def route_tokens(
    features, cotangent, tenant_ids, document_index_per_token, owner_map, adapter_down, adapter_up
):
    ranks = lax.axis_size("dp")
    rows = features.shape[0]
    width = features.shape[1]
    capacity = max(2, 2 * rows // ranks)
    slots = ranks * capacity
    token_row_index = jnp.arange(rows, dtype=jnp.int32)
    target = token_owner(tenant_ids, owner_map)
    routing_weight = token_weight(document_index_per_token)
    earlier = (token_row_index[:, None] > token_row_index[None, :]) & (
        target[:, None] == target[None, :]
    )
    before = jnp.sum(earlier.astype(jnp.int32), axis=1)
    slot_of = target * capacity + before
    placed = slot_of[None, :] == jnp.arange(slots, dtype=jnp.int32)[:, None]
    slot_weight = jnp.sum(
        jnp.where(placed, routing_weight[None, :], jnp.zeros_like(routing_weight)[None, :]), axis=1
    )

    def pack(values):
        return jnp.dot(
            placed.astype(values.dtype), values, preferred_element_type=jnp.float32
        ).astype(values.dtype)

    def exchange(values):
        return lax.all_to_all(values, "dp", split_axis=0, concat_axis=0, tiled=True)

    down_own = adapter_down[0]
    up_own = adapter_up[0]
    got_x = exchange(pack(features).reshape(ranks, capacity, width)).reshape(slots, width)
    got_g = exchange(pack(cotangent).reshape(ranks, capacity, width)).reshape(slots, width)
    got_w = exchange(slot_weight.reshape(ranks, capacity)).reshape(slots)
    low_h, low_u = lax.psum(
        (contract_last(got_x, down_own), contract_last(got_g, up_own)), "tensor"
    )
    scaled_h = (low_h * got_w[:, None]).astype(jnp.bfloat16)
    scaled_u = (low_u * got_w[:, None]).astype(jnp.bfloat16)
    up_adapter_gradient = contract_first(scaled_h, got_g)
    grad_down = contract_first(scaled_u, got_x)
    slot_dx = jnp.dot(scaled_u, down_own, preferred_element_type=jnp.float32).astype(jnp.bfloat16)
    returned = exchange(slot_dx.reshape(ranks, capacity, width)).reshape(slots, width)
    input_grad = contract_first(placed.astype(jnp.bfloat16), returned).astype(jnp.bfloat16)
    return (input_grad, grad_down[None], up_adapter_gradient[None])


VMEM_LIMIT = 32 * 1024 * 1024


def whole(*shape):
    return pl.BlockSpec(shape, lambda _: (0,) * len(shape))


def column_cut(rows, wide, at):
    return pl.BlockSpec((rows, wide), lambda _: (0, at))


def cost(flops, moved):
    if CFG['zero']:
        flops = moved = 0
    return pl.CostEstimate(flops=flops, bytes_accessed=moved, transcendentals=0)


def join_kernel(layer_ref, own_ref, *refs):
    *halves, out_ref = refs
    count = len(halves) // 2
    rank = own_ref.shape[0]
    out_ref[:rank, :] = own_ref[...]
    first = layer_ref[0] == 0
    for step in range(count):
        got, other = halves[step][...], halves[count + step][...]
        low = (step + 1) * rank
        middle = low + rank // 2
        out_ref[low:middle, :] = jnp.where(first, got, other)
        out_ref[middle : low + rank, :] = jnp.where(first, other, got)


def join(layer, own, got, other, at=0):
    rank, width = own.shape
    rows = (len(got) + 1) * rank
    return pl.pallas_call(
        join_kernel,
        grid=(1,),
        out_shape=jax.ShapeDtypeStruct((rows, width), own.dtype),
        in_specs=[pl.BlockSpec(memory_space=pltpu.SMEM), whole(rank, width)]
        + [pl.BlockSpec((rank // 2, width), lambda _: (at, 0))] * (2 * len(got)),
        out_specs=whole(rows, width),
        compiler_params=pltpu.CompilerParams(vmem_limit_bytes=VMEM_LIMIT),
        cost_estimate=cost(0, 4 * rows * width),
    )(layer, own, *got, *other)


def stack_kernel(*refs):
    *parts, out_ref = refs
    rank = parts[0].shape[0]
    for at, part in enumerate(parts):
        out_ref[at * rank : (at + 1) * rank, :] = part[...]


def stack_rows(parts):
    rank, width = parts[0].shape
    return pl.pallas_call(
        stack_kernel,
        grid=(1,),
        out_shape=jax.ShapeDtypeStruct((rank * len(parts), width), parts[0].dtype),
        in_specs=[whole(rank, width)] * len(parts),
        out_specs=whole(rank * len(parts), width),
        compiler_params=pltpu.CompilerParams(vmem_limit_bytes=VMEM_LIMIT),
        cost_estimate=cost(0, 4 * rank * len(parts) * width),
    )(*parts)


def project_kernel(adapter_ref, own_ref, other_ref, held_ref, base_ref, out_ref):
    columns, tokens = held_ref.shape
    rows = tokens // 2
    rank = adapter_ref.shape[0] // columns
    adapters = adapter_ref[...]
    for part, rows_ref in enumerate((own_ref, other_ref)):
        cut = slice(part * rows, (part + 1) * rows)
        low = contract_last(adapters, rows_ref[...])
        total = base_ref[:, cut]
        for step in range(columns):
            total = total + jnp.where(
                held_ref[step : step + 1, cut] > 0, low[step * rank : (step + 1) * rank], 0.0
            )
        out_ref[:, cut] = total


def project(adapters, own_rows, other_rows, held, base, at):
    rows, wide = other_rows.shape
    height = adapters.shape[0]
    return pl.pallas_call(
        project_kernel,
        grid=(1,),
        out_shape=jax.ShapeDtypeStruct(base.shape, jnp.float32),
        in_specs=[
            column_cut(height, wide, at),
            column_cut(rows, wide, at),
            whole(rows, wide),
            whole(*held.shape),
            whole(*base.shape),
        ],
        out_specs=whole(*base.shape),
        compiler_params=pltpu.CompilerParams(vmem_limit_bytes=VMEM_LIMIT),
        cost_estimate=cost(4 * height * rows * wide, 2 * wide * (height + 2 * rows)),
    )(adapters, own_rows, other_rows, held, base)


def partial_kernel(keep, away, scaled_ref, held_ref, own_ref, other_ref, keep_ref, *away_refs):
    columns, tokens = held_ref.shape
    rows = tokens // 2
    rank = scaled_ref.shape[0]
    scaled = scaled_ref[...]
    left = jnp.concatenate(
        [
            jnp.where(held_ref[step : step + 1, :] > 0, scaled, 0.0).astype(jnp.bfloat16)
            for step in range(columns)
        ]
    )
    total = jnp.dot(left[:, :rows], own_ref[...], preferred_element_type=jnp.float32)
    total = total + jnp.dot(left[:, rows:], other_ref[...], preferred_element_type=jnp.float32)
    for group, out_ref in zip((keep,) + away, (keep_ref,) + away_refs):
        for at, block in enumerate(group):
            out_ref[at * rank : (at + 1) * rank, :] = total[
                block * rank : (block + 1) * rank
            ].astype(out_ref.dtype)


def partials(scaled, held, own_rows, other_rows, at, keep, away, kind=jnp.float32, wide=None):
    columns, tokens = held.shape
    rows = other_rows.shape[0]
    there_at = at if wide else 0
    wide = wide or other_rows.shape[1]
    rank = scaled.shape[0]
    shapes = [(len(group) * rank, wide) for group in (keep,) + away]
    return pl.pallas_call(
        functools.partial(partial_kernel, keep, away),
        grid=(1,),
        out_shape=[jax.ShapeDtypeStruct(shapes[0], kind)]
        + [jax.ShapeDtypeStruct(shape, jnp.bfloat16) for shape in shapes[1:]],
        in_specs=[
            whole(*scaled.shape),
            whole(*held.shape),
            column_cut(rows, wide, at),
            column_cut(rows, wide, there_at),
        ],
        out_specs=[whole(*shape) for shape in shapes],
        compiler_params=pltpu.CompilerParams(vmem_limit_bytes=VMEM_LIMIT),
        cost_estimate=cost(2 * columns * rank * tokens * wide, 8 * rows * wide),
    )(scaled, held, own_rows, other_rows)


def sums_into(out_ref, rank, cuts, refs):
    refs = list(refs)
    for start, wide, count in cuts:
        first = refs.pop(0)
        total = first[:rank, :].astype(jnp.float32)
        if count == 1:
            for at in range(1, first.shape[0] // rank):
                total = total + first[at * rank : (at + 1) * rank, :].astype(jnp.float32)
        for _ in range(count - 1):
            total = total + refs.pop(0)[:rank, :].astype(jnp.float32)
        out_ref[0, :, start : start + wide] = total


def dx_into(dx_ref, low_ref, low_there_ref, held_ref, held_there_ref, down_ref, there_ref):
    left = jnp.concatenate(
        [
            jnp.where(mask_ref[step : step + 1, :] > 0, low[...], 0.0).astype(jnp.bfloat16)
            for low, mask_ref in ((low_ref, held_ref), (low_there_ref, held_there_ref))
            for step in range(held_ref.shape[0])
        ]
    )
    half = down_ref.shape[0]
    dx = contract_first(left[:half], down_ref[...]) + contract_first(left[half:], there_ref[...])
    dx_ref[...] = dx.astype(dx_ref.dtype)


def finish_kernel(rank, dx, groups, *refs):
    refs = list(refs)
    ins = [refs[: (6 if dx else 0)]]
    del refs[: (6 if dx else 0)]
    for cuts in groups:
        count = sum(cut[2] for cut in cuts)
        ins.append(refs[:count])
        del refs[:count]
    if dx:
        dx_into(refs.pop(0), *ins[0])
    for cuts, group, out_ref in zip(groups, ins[1:], refs):
        sums_into(out_ref, rank, cuts, group)


def finish(rank, width, dx_operands, groups):
    operands, cuts, shapes = list(dx_operands), [], []
    if dx_operands:
        shapes.append(jax.ShapeDtypeStruct((dx_operands[0].shape[1], width), jnp.bfloat16))
    for group in groups:
        cuts.append([(start, wide, len(parts)) for start, wide, parts in group])
        for _, _, parts in group:
            operands.extend(parts)
        shapes.append(jax.ShapeDtypeStruct((1, rank, width), jnp.float32))
    return pl.pallas_call(
        functools.partial(finish_kernel, rank, bool(dx_operands), cuts),
        grid=(1,),
        out_shape=shapes,
        in_specs=[whole(*operand.shape) for operand in operands],
        out_specs=[whole(*shape.shape) for shape in shapes],
        compiler_params=pltpu.CompilerParams(vmem_limit_bytes=VMEM_LIMIT),
        cost_estimate=cost(4 * 128 * 128 * width, 32 * rank * width),
    )(*operands)


def split_kernel(cuts, scaled_ref, held_ref, own_ref, other_ref, *out_refs):
    columns, tokens = held_ref.shape
    rows = tokens // 2
    rank = scaled_ref.shape[0]
    scaled = scaled_ref[...]
    left = jnp.concatenate(
        [
            jnp.where(held_ref[step : step + 1, :] > 0, scaled, 0.0).astype(jnp.bfloat16)
            for step in range(columns)
        ]
    )
    for i, (start, wide) in enumerate(cuts):
        cut = slice(start, start + wide)
        total = jnp.dot(left[:, :rows], own_ref[:, cut], preferred_element_type=jnp.float32)
        total = total + jnp.dot(
            left[:, rows:], other_ref[:, cut], preferred_element_type=jnp.float32
        )
        for out_ref, blocks in zip(out_refs[2 * i : 2 * i + 2], ((0, 2), (1, 3))):
            for at, block in enumerate(blocks):
                out_ref[at * rank : (at + 1) * rank, :] = total[
                    block * rank : (block + 1) * rank
                ].astype(out_ref.dtype)


def split_partials(scaled, held, own_rows, other_rows, cuts):
    columns, tokens = held.shape
    rows, width = other_rows.shape
    rank = scaled.shape[0]
    shapes = []
    for _, wide in cuts:
        shapes.append(jax.ShapeDtypeStruct((2 * rank, wide), jnp.float32))
        shapes.append(jax.ShapeDtypeStruct((2 * rank, wide), jnp.bfloat16))
    return pl.pallas_call(
        functools.partial(split_kernel, cuts),
        grid=(1,),
        out_shape=shapes,
        in_specs=[
            whole(*scaled.shape),
            whole(*held.shape),
            whole(rows, width),
            whole(rows, width),
        ],
        out_specs=[whole(*shape.shape) for shape in shapes],
        compiler_params=pltpu.CompilerParams(vmem_limit_bytes=VMEM_LIMIT),
        cost_estimate=cost(2 * columns * rank * tokens * width, 8 * rows * width),
    )(scaled, held, own_rows, other_rows)


def route_adapters(
    features, cotangent, tenant_ids, document_index_per_token, owner_map, adapter_down, adapter_up
):
    ranks = lax.axis_size("dp")
    columns = ranks // 2
    rows, width = features.shape
    rank = adapter_down.shape[1]
    half = rank // 2
    me = lax.axis_index("dp")
    side, place = me % 2, me // 2
    layer = lax.axis_index("parts")

    def swap_side(value):
        return lax.ppermute(value, "dp", [(i, i ^ 1) for i in range(ranks)])

    def hop(value, by):
        return lax.ppermute(value, "dp", [(i, i ^ (2 * by)) for i in range(ranks)])

    def swap_layer(value):
        return lax.ppermute(value, "parts", [(0, 1), (1, 0)])

    def swap_core(value):
        return lax.ppermute(value, "tensor", [(0, 1), (1, 0)])

    def half_rows(own):
        return lax.dynamic_slice(own, (layer * half, 0), (half, width))

    def fetch(own):
        order = CFG["zorder"]
        got = {step: hop(own, step) for step in order}
        return [got[step] for step in range(1, columns)]

    def add(total, *got):
        for block in got:
            total = total + block.astype(jnp.float32)
        return total

    cuts = CFG["cuts"]
    eighth = width // 8
    layer_of = layer.astype(jnp.int32)[None]
    other_x = swap_side(features)
    ids_there = swap_side(jnp.stack([tenant_ids, document_index_per_token]))
    down_own, up_own = adapter_down[0], adapter_up[0]
    if CFG["a_ids_first"]:
        down_own = after(down_own, ids_there)

    def exchange(got, mode, tie2=(), tie3=()):
        if mode == "y1":
            other = swap_layer(jnp.stack([after(got[0], *tie2)] + got[1:]))
            return got, list(other)
        if CFG["a_y2"]:
            got[1] = after(got[1], *tie2)
        other = [swap_layer(block) for block in got[:2]]
        deps = tuple(tie3)
        if CFG["a_y3y1"]:
            deps += (other[0],)
        if deps:
            got[2] = after(got[2], *deps)
        other.append(swap_layer(got[2]))
        return got, other

    own_g = [cotangent[:, i * eighth : (i + n) * eighth] for i, n in cuts]
    tie3 = (other_x,) if CFG["a_y3x"] else ()
    if CFG["fetch"] == "both":
        src = jnp.concatenate([half_rows(down_own), half_rows(up_own)])
        got = fetch(src)
        if CFG["a_slice"]:
            got[1], *own_g = lax.optimization_barrier((got[1], *own_g))
        got, other = exchange(got, CFG["ya"], (), tie3)
        down = join(layer_of, down_own, got, other, 0)
        up = join(layer_of, up_own, got, other, 1)
        up_got = got
    else:
        if CFG["fetch"] == "full":
            down_got = fetch(down_own)
            down = stack_rows([down_own] + down_got)
        else:
            down_got = fetch(half_rows(down_own))
            if CFG["a_slice"]:
                down_got[1], *own_g = lax.optimization_barrier((down_got[1], *own_g))
            if CFG["a_bz"]:
                up_got = fetch(half_rows(after(up_own, down_got[0]) if CFG["a_up"] else up_own))
                tie3 += tuple(up_got)
            down_got, down_other = exchange(down_got, CFG["ya"], (), tie3)
            down = join(layer_of, down_own, down_got, down_other)
        if CFG["a_up"] == "z":
            up_own = after(up_own, down_got[0])
        elif CFG["a_up"] == "y":
            up_own = after(up_own, down)
        if CFG["fetch"] == "full" or not CFG["a_bz"]:
            up_got = fetch(half_rows(up_own))
        up_gots = list(up_got)
        if CFG["a_upy"]:
            up_gots[0] = after(up_gots[0], down)
        up_gots, up_other = exchange(up_gots, CFG["yb"])
        up = join(layer_of, up_own, up_gots, up_other)
    if CFG["a_idsdown"]:
        ids_there = after(ids_there, down)
    if CFG["a_g"]:
        own_g[0] = after(own_g[0], down_got[0] if CFG["fetch"] != "both" else up_got[0])
    line = [other_x]
    for i, cut in enumerate(own_g):
        back_by = CFG["a_chain"]
        if back_by and i + 1 >= back_by:
            cut = after(cut, line[i + 1 - back_by])
        line.append(swap_side(cut))
    other_g = line[1:]

    owner, owner_there = token_owner(tenant_ids, owner_map), token_owner(ids_there[0], owner_map)
    weight = token_weight(document_index_per_token)
    owner_here = jnp.concatenate([owner, owner_there])
    weight_here = jnp.concatenate([weight, token_weight(ids_there[1])])
    steps = jnp.arange(columns, dtype=jnp.int32)
    block_owner = (place ^ steps) * 2 + side
    block_owner_there = block_owner + 1 - 2 * side
    held = (block_owner[:, None] == owner_here[None, :]).astype(jnp.float32)
    plain = steps * 2 + side
    held_plain = (plain[:, None] == owner_here[None, :]).astype(jnp.float32)
    own_held = (block_owner[:, None] == owner[None, :]).astype(jnp.float32)
    own_there = (block_owner_there[:, None] == owner[None, :]).astype(jnp.float32)

    def combine(low):
        return ((low + swap_core(low)) * weight_here[None, :]).astype(jnp.bfloat16)

    nothing = jnp.zeros((rank, 2 * rows), jnp.float32)
    x_in = after(other_x, *up_got) if CFG["a_xup"] else other_x
    if CFG["a_xg"]:
        x_in = after(x_in, *other_g[: CFG["a_xg"]])
    scaled_h = combine(project(down, features, x_in, held, nothing, 0))
    if CFG["a_g0up"] is not None:
        at = min(CFG["a_g0up"], len(cuts) - 1)
        other_g[at] = after(other_g[at], up)

    def scatter(scaled, own_rows, there, start, count, mode, full=False):
        at = start // count
        wide = count * eighth if full else None
        if mode == "a2a":
            (away,) = partials(scaled, held_plain, own_rows, there, at, (0, 1, 2, 3), (), jnp.bfloat16, wide)
            wide = away.shape[1]
            got = lax.all_to_all(
                away.reshape(columns, rank, wide), "dp", split_axis=0, concat_axis=0, tiled=True,
                axis_index_groups=[list(range(s, ranks, 2)) for s in range(2)],
            )
            return away, [got.reshape(columns * rank, wide)]
        if mode == "dd":
            total, away = partials(scaled, held, own_rows, there, at, (0, 2), ((1, 3),), wide=wide)
            return total, [total, hop(away, 1)]
        total, *blocks = partials(scaled, held, own_rows, there, at, (0,), ((1,), (2,), (3,)), wide=wide)
        order = CFG["sorder"]
        got = {step: hop(blocks[step - 1], step) for step in order}
        return total, [total] + [got[step] for step in order]

    def forward(parts, *deps):
        total, first = parts
        here = after(first, *deps) if deps else first
        src = add(total[rank:], here[rank:]).astype(jnp.bfloat16)
        srcs.append(src)
        return [total, first, hop(src, 2)]

    srcs = []
    low_u = nothing
    up_group = []
    waits = CFG["s2"]
    for i, (start, count) in enumerate(cuts):
        there = other_g[i]
        if i >= 1 and CFG["a_prev"]:
            there = after(there, up_group[i - 1][2][-1])
        if i >= 2 and CFG["a_prev2"] and (CFG["db"] != "dd" or waits[i - 2] == 0):
            there = after(there, *up_group[i - 2][2])
        if CFG["late_b"] and i == len(cuts) - 1:
            up_group.append((start * eighth, count * eighth, None))
        else:
            total, parts = scatter(scaled_h, cotangent, there, start, count, CFG["db"])
            if CFG["db"] == "dd" and waits[i] == 0:
                parts = forward(parts)
            up_group.append((start * eighth, count * eighth, parts))
            if CFG["a_pu"]:
                there = after(there, total)
        low_u = project(up, cotangent, there, held, low_u, start // count)
    if CFG["a_last"]:
        low_u = after(low_u, *up_group[CFG["a_last"] - 1][2])
    if CFG["db"] == "dd":
        for i in range(len(cuts)):
            if waits[i] == 1 and up_group[i][2]:
                up_group[i] = up_group[i][:2] + (forward(up_group[i][2], low_u),)
    scaled_u = combine(low_u)
    if CFG["a_su"]:
        scaled_u = after(scaled_u, *srcs)
    down_group = []
    last = None
    if CFG["da"] == "split":
        outs = split_partials(
            scaled_u, held, features, other_x,
            tuple((start * eighth, count * eighth) for start, count in CFG["xcuts"]),
        )
        total = outs[0]
        for i, (start, count) in enumerate(CFG["xcuts"]):
            parts = [outs[2 * i], hop(outs[2 * i + 1], 1)]
            down_group.append((start * eighth, count * eighth, parts))
    for start, count in CFG["xcuts"] if CFG["da"] != "split" else ():
        total, parts = scatter(scaled_u, features, other_x, start, count, CFG["da"], True)
        down_group.append((start * eighth, count * eighth, parts))
    if CFG["late_b"]:
        start, count = cuts[-1]
        _, parts = scatter(scaled_h, cotangent, after(other_g[-1], total), start, count, CFG["db"])
        if CFG["late_b"] == 2:
            parts = forward(parts)
            waits = waits[: len(cuts) - 1] + (0,)
        up_group[-1] = up_group[-1][:2] + (parts,)
    if CFG["da"] in ("dd", "split"):
        down_group = [group[:2] + (forward(group[2]),) for group in down_group]
    if CFG["db"] == "dd":
        for i in range(len(cuts)):
            if waits[i] == 2:
                up_group[i] = up_group[i][:2] + (forward(up_group[i][2], total),)
            if waits[i] == 3:
                up_group[i] = up_group[i][:2] + (forward(up_group[i][2], down_group[0][2][-1]),)
    back_src = scaled_u
    if CFG["a_back"] == "late":
        back_src = after(scaled_u, srcs[-1])
    elif CFG["a_back"]:
        back_src = after(scaled_u, total)
    back = swap_side(back_src[:, rows:])
    down_there = swap_side(after(down, line[CFG["a_there"]]) if CFG["a_there"] is not None else down)
    if CFG["a_backgot"] == "all":
        back = after(back, *[part for group in down_group for part in group[2]])
    elif CFG["a_backgot"] is not None:
        back = after(back, down_group[0][2][-1])
    dx_ops = (scaled_u[:, :rows], back, own_held, own_there, down, down_there)
    if CFG["fin"] == "one":
        return finish(rank, width, dx_ops, [down_group, up_group])
    if CFG["fin"] == "two":
        (up_grad,) = finish(rank, width, (), [up_group])
        return finish(rank, width, dx_ops, [down_group]) + [up_grad]
    (up_grad,) = finish(rank, width, (), [up_group])
    (dx,) = finish(rank, width, dx_ops, [])
    s0, c0, p0 = down_group[-1]
    down_group[-1] = (s0, c0, p0[:-1] + [after(p0[-1], dx)])
    (down_grad,) = finish(rank, width, (), [down_group])
    return dx, down_grad, up_grad


def shards(features, *others):
    ranks = lax.axis_size("dp")
    rank = others[-1].shape[1]
    slots = 2 * features.shape[0] // ranks
    fits = rank % 32 == 0 and features.shape[1] % 1024 == 0
    if slots >= rank and fits and ranks == 8 and lax.axis_size("parts") == 2:
        return route_adapters(features, *others)
    return route_tokens(features, *others)


def solution(mesh):
    return jax.shard_map(
        shards,
        mesh=mesh,
        in_specs=(
            P(("parts", "dp"), "tensor"),
            P(("parts", "dp"), "tensor"),
            P(("parts", "dp")),
            P(("parts", "dp")),
            P(),
            P("dp", None, "tensor"),
            P("dp", None, "tensor"),
        ),
        out_specs=(
            P(("parts", "dp"), "tensor"),
            P(("parts", "dp"), None, "tensor"),
            P(("parts", "dp"), None, "tensor"),
        ),
        check_vma=False,
    )
```

```python
import jax
import jax.numpy as jnp
from jax import lax
from jax.experimental import pallas as pl
from jax.experimental.pallas import tpu as pltpu
from jax.sharding import PartitionSpec as P

adapter_scale_factor = 2.0


def contract_last(left, right):
    return lax.dot_general(
        left, right, (((1,), (1,)), ((), ())), preferred_element_type=jnp.float32
    )


def contract_first(left, right):
    return lax.dot_general(
        left, right, (((0,), (0,)), ((), ())), preferred_element_type=jnp.float32
    )


def token_owner(tenant_ids, owner_map):
    tenant_total = owner_map.shape[0]
    match = tenant_ids[:, None] == jnp.arange(tenant_total, dtype=jnp.int32)[None, :]
    return jnp.sum(jnp.where(match, owner_map[None, :], 0), axis=1)


def token_weight(document_index_per_token):
    same_doc = document_index_per_token[:, None] == document_index_per_token[None, :]
    sequence_length = jnp.sum(same_doc.astype(jnp.float32), axis=1)
    return adapter_scale_factor / sequence_length


def after(value, *others):
    return lax.optimization_barrier((value,) + others)[0]


def route_tokens(
    features, cotangent, tenant_ids, document_index_per_token, owner_map, adapter_down, adapter_up
):
    ranks = lax.axis_size("dp")
    rows = features.shape[0]
    width = features.shape[1]
    capacity = max(2, 2 * rows // ranks)
    slots = ranks * capacity
    token_row_index = jnp.arange(rows, dtype=jnp.int32)
    target = token_owner(tenant_ids, owner_map)
    routing_weight = token_weight(document_index_per_token)
    earlier = (token_row_index[:, None] > token_row_index[None, :]) & (
        target[:, None] == target[None, :]
    )
    before = jnp.sum(earlier.astype(jnp.int32), axis=1)
    slot_of = target * capacity + before
    placed = slot_of[None, :] == jnp.arange(slots, dtype=jnp.int32)[:, None]
    slot_weight = jnp.sum(
        jnp.where(placed, routing_weight[None, :], jnp.zeros_like(routing_weight)[None, :]), axis=1
    )

    def pack(values):
        return jnp.dot(
            placed.astype(values.dtype), values, preferred_element_type=jnp.float32
        ).astype(values.dtype)

    def exchange(values):
        return lax.all_to_all(values, "dp", split_axis=0, concat_axis=0, tiled=True)

    down_own = adapter_down[0]
    up_own = adapter_up[0]
    got_x = exchange(pack(features).reshape(ranks, capacity, width)).reshape(slots, width)
    got_g = exchange(pack(cotangent).reshape(ranks, capacity, width)).reshape(slots, width)
    got_w = exchange(slot_weight.reshape(ranks, capacity)).reshape(slots)
    low_h, low_u = lax.psum(
        (contract_last(got_x, down_own), contract_last(got_g, up_own)), "tensor"
    )
    scaled_h = (low_h * got_w[:, None]).astype(jnp.bfloat16)
    scaled_u = (low_u * got_w[:, None]).astype(jnp.bfloat16)
    up_adapter_gradient = contract_first(scaled_h, got_g)
    grad_down = contract_first(scaled_u, got_x)
    slot_dx = jnp.dot(scaled_u, down_own, preferred_element_type=jnp.float32).astype(jnp.bfloat16)
    returned = exchange(slot_dx.reshape(ranks, capacity, width)).reshape(slots, width)
    input_grad = contract_first(placed.astype(jnp.bfloat16), returned).astype(jnp.bfloat16)
    return (input_grad, grad_down[None], up_adapter_gradient[None])


VMEM_LIMIT = 32 * 1024 * 1024


def whole(*shape):
    return pl.BlockSpec(shape, lambda _: (0,) * len(shape))


def column_cut(rows, wide, at):
    return pl.BlockSpec((rows, wide), lambda _: (0, at))


def small_kernel(kernel, out_shape, in_specs, out_specs):
    return pl.pallas_call(
        kernel,
        grid=(1,),
        out_shape=out_shape,
        in_specs=in_specs,
        out_specs=out_specs,
        compiler_params=pltpu.CompilerParams(vmem_limit_bytes=VMEM_LIMIT),
        cost_estimate=pl.CostEstimate(flops=0, bytes_accessed=0, transcendentals=0),
    )


def spread(scaled, held_ref):
    return jnp.concatenate(
        [
            jnp.where(held_ref[step : step + 1, :] > 0, scaled, 0.0).astype(jnp.bfloat16)
            for step in range(held_ref.shape[0])
        ]
    )


def join_kernel(layer_ref, own_ref, *refs):
    *halves, out_ref = refs
    count = len(halves) // 2
    rank = own_ref.shape[0]
    out_ref[:rank, :] = own_ref[...]
    first = layer_ref[0] == 0
    for step in range(count):
        got, other = halves[step][...], halves[count + step][...]
        low = (step + 1) * rank
        middle = low + rank // 2
        out_ref[low:middle, :] = jnp.where(first, got, other)
        out_ref[middle : low + rank, :] = jnp.where(first, other, got)


def join(layer, own, got, other):
    rank, width = own.shape
    rows = (len(got) + 1) * rank
    return small_kernel(
        join_kernel,
        jax.ShapeDtypeStruct((rows, width), own.dtype),
        [pl.BlockSpec(memory_space=pltpu.SMEM), whole(rank, width)]
        + [whole(rank // 2, width)] * (2 * len(got)),
        whole(rows, width),
    )(layer, own, *got, *other)


def project_kernel(adapter_ref, own_ref, other_ref, held_ref, base_ref, out_ref):
    columns, tokens = held_ref.shape
    rows = tokens // 2
    rank = adapter_ref.shape[0] // columns
    adapters = adapter_ref[...]
    for part, rows_ref in enumerate((own_ref, other_ref)):
        cut = slice(part * rows, (part + 1) * rows)
        low = contract_last(adapters, rows_ref[...])
        total = base_ref[:, cut]
        for step in range(columns):
            total = total + jnp.where(
                held_ref[step : step + 1, cut] > 0, low[step * rank : (step + 1) * rank], 0.0
            )
        out_ref[:, cut] = total


def project(adapters, own_rows, other_rows, held, base, at):
    rows, wide = other_rows.shape
    return small_kernel(
        project_kernel,
        jax.ShapeDtypeStruct(base.shape, jnp.float32),
        [
            column_cut(adapters.shape[0], wide, at),
            column_cut(rows, wide, at),
            whole(rows, wide),
            whole(*held.shape),
            whole(*base.shape),
        ],
        whole(*base.shape),
    )(adapters, own_rows, other_rows, held, base)


def partial_kernel(scaled_ref, held_ref, own_ref, other_ref, *out_refs):
    rows = own_ref.shape[0]
    rank = scaled_ref.shape[0]
    left = spread(scaled_ref[...], held_ref)
    wide = out_refs[0].shape[1]
    for i in range(len(out_refs) // 2):
        cut = slice(i * wide, (i + 1) * wide)
        total = jnp.dot(left[:, :rows], own_ref[:, cut], preferred_element_type=jnp.float32)
        total = total + jnp.dot(
            left[:, rows:], other_ref[:, cut], preferred_element_type=jnp.float32
        )
        for out_ref, blocks in zip(out_refs[2 * i : 2 * i + 2], ((0, 2), (1, 3))):
            for at, block in enumerate(blocks):
                out_ref[at * rank : (at + 1) * rank, :] = total[
                    block * rank : (block + 1) * rank
                ].astype(out_ref.dtype)


def partials(scaled, held, own_rows, other_rows, at, pieces):
    rows, wide = other_rows.shape
    shape = (2 * scaled.shape[0], wide // pieces)
    kinds = [jnp.float32, jnp.bfloat16] * pieces
    return small_kernel(
        partial_kernel,
        [jax.ShapeDtypeStruct(shape, kind) for kind in kinds],
        [
            whole(*scaled.shape),
            whole(*held.shape),
            column_cut(rows, wide, at),
            whole(rows, wide),
        ],
        [whole(*shape)] * len(kinds),
    )(scaled, held, own_rows, other_rows)


def add_kernel(*refs):
    *parts, out_ref = refs
    rank = out_ref.shape[1]
    wide = parts[0].shape[1]
    for i in range(len(parts) // 3):
        total = parts[3 * i][:rank, :]
        for part in parts[3 * i + 1 : 3 * i + 3]:
            total = total + part[:rank, :].astype(jnp.float32)
        out_ref[0, :, i * wide : (i + 1) * wide] = total


def add_parts(groups, rank, width):
    operands = [part for group in groups for part in group]
    return small_kernel(
        add_kernel,
        jax.ShapeDtypeStruct((1, rank, width), jnp.float32),
        [whole(*operand.shape) for operand in operands],
        whole(1, rank, width),
    )(*operands)


def input_grad_kernel(low_ref, low_there_ref, held_ref, held_there_ref, down_ref, there_ref, dx_ref):
    dx = contract_first(spread(low_ref[...], held_ref), down_ref[...])
    dx = dx + contract_first(spread(low_there_ref[...], held_there_ref), there_ref[...])
    dx_ref[...] = dx.astype(dx_ref.dtype)


def input_gradient(*operands):
    shape = (operands[0].shape[1], operands[-1].shape[1])
    return small_kernel(
        input_grad_kernel,
        jax.ShapeDtypeStruct(shape, jnp.bfloat16),
        [whole(*operand.shape) for operand in operands],
        whole(*shape),
    )(*operands)


def route_adapters(
    features, cotangent, tenant_ids, document_index_per_token, owner_map, adapter_down, adapter_up
):
    ranks = lax.axis_size("dp")
    columns = ranks // 2
    rows, width = features.shape
    rank = adapter_down.shape[1]
    half = rank // 2
    me = lax.axis_index("dp")
    side, place = me % 2, me // 2
    layer = lax.axis_index("parts")

    def swap_side(value):
        return lax.ppermute(value, "dp", [(i, i ^ 1) for i in range(ranks)])

    def hop(value, by):
        return lax.ppermute(value, "dp", [(i, i ^ (2 * by)) for i in range(ranks)])

    def swap_layer(value):
        return lax.ppermute(value, "parts", [(0, 1), (1, 0)])

    def swap_core(value):
        return lax.ppermute(value, "tensor", [(0, 1), (1, 0)])

    def fetch(own):
        mine = lax.dynamic_slice(own, (layer * half, 0), (half, width))
        got = {step: hop(mine, step) for step in range(columns - 1, 0, -1)}
        return [got[step] for step in range(1, columns)]

    pieces = 2
    wide = width // pieces
    layer_of = layer.astype(jnp.int32)[None]
    other_x = swap_side(features)
    ids_there = swap_side(jnp.stack([tenant_ids, document_index_per_token]))
    down_own = after(adapter_down[0], ids_there)
    own_g = [cotangent[:, i * wide : (i + 1) * wide] for i in range(pieces)]
    down_got = fetch(down_own)
    down = join(layer_of, down_own, down_got, [swap_layer(got) for got in down_got])
    up_own = after(adapter_up[0], down_got[0])
    up_got = fetch(up_own)
    up_halves = [after(up_got[0], down)] + up_got[1:]
    up = join(layer_of, up_own, up_halves, [swap_layer(got) for got in up_halves])
    ids_there = after(ids_there, down)
    other_g = [swap_side(cut) for cut in own_g]

    owner, owner_there = token_owner(tenant_ids, owner_map), token_owner(ids_there[0], owner_map)
    weight = token_weight(document_index_per_token)
    owner_here = jnp.concatenate([owner, owner_there])
    weight_here = jnp.concatenate([weight, token_weight(ids_there[1])])
    block_owner = (place ^ jnp.arange(columns, dtype=jnp.int32)) * 2 + side
    block_owner_there = block_owner + 1 - 2 * side
    held = (block_owner[:, None] == owner_here[None, :]).astype(jnp.float32)
    own_held = (block_owner[:, None] == owner[None, :]).astype(jnp.float32)
    own_there = (block_owner_there[:, None] == owner[None, :]).astype(jnp.float32)

    def combine(low):
        return ((low + swap_core(low)) * weight_here[None, :]).astype(jnp.bfloat16)

    def second_block(kept, came):
        return (kept[rank:] + came[rank:].astype(jnp.float32)).astype(jnp.bfloat16)

    nothing = jnp.zeros((rank, 2 * rows), jnp.float32)
    x_in = after(after(other_x, *up_got), other_g[0])
    scaled_h = combine(project(down, features, x_in, held, nothing, 0))

    first_g = after(other_g[0], up)
    kept, away = partials(scaled_h, held, cotangent, first_g, 0, 1)
    came = hop(away, 1)
    onward = second_block(kept, came)
    up_groups = [(kept, came, hop(onward, 2))]
    low_u = project(up, cotangent, after(first_g, kept), held, nothing, 0)
    low_u = project(up, cotangent, other_g[1], held, low_u, 1)
    scaled_u = after(combine(low_u), onward)

    outs = partials(scaled_u, held, features, other_x, 0, pieces)
    down_kept, down_came = outs[0::2], [hop(away, 1) for away in outs[1::2]]
    kept, away = partials(scaled_h, held, cotangent, after(other_g[1], outs[0]), 1, 1)
    came = hop(away, 1)
    down_groups = [
        (kept_x, came_x, hop(second_block(kept_x, came_x), 2))
        for kept_x, came_x in zip(down_kept, down_came)
    ]
    onward = second_block(kept, after(came, outs[0]))
    up_groups.append((kept, came, hop(onward, 2)))
    back = swap_side(after(scaled_u, onward)[:, rows:])
    down_there = swap_side(after(down, other_g[1]))
    up_adapter_gradient = add_parts(up_groups, rank, width)
    input_grad = input_gradient(scaled_u[:, :rows], back, own_held, own_there, down, down_there)
    kept, came, last = down_groups[-1]
    down_groups[-1] = (kept, came, after(last, input_grad))
    grad_down = add_parts(down_groups, rank, width)
    return (input_grad, grad_down, up_adapter_gradient)


def shards(features, *others):
    ranks = lax.axis_size("dp")
    rank = others[-1].shape[1]
    slots = 2 * features.shape[0] // ranks
    fits = rank % 32 == 0 and features.shape[1] % 1024 == 0
    if slots >= rank and fits and ranks == 8 and lax.axis_size("parts") == 2:
        return route_adapters(features, *others)
    return route_tokens(features, *others)


def solution(mesh):
    return jax.shard_map(
        shards,
        mesh=mesh,
        in_specs=(
            P(("parts", "dp"), "tensor"),
            P(("parts", "dp"), "tensor"),
            P(("parts", "dp")),
            P(("parts", "dp")),
            P(),
            P("dp", None, "tensor"),
            P("dp", None, "tensor"),
        ),
        out_specs=(
            P(("parts", "dp"), "tensor"),
            P(("parts", "dp"), None, "tensor"),
            P(("parts", "dp"), None, "tensor"),
        ),
        check_vma=False,
    )
```

```python
import jax
import jax.numpy as jnp
from jax import lax
from jax.experimental import pallas as pl
from jax.experimental.pallas import tpu as pltpu
from jax.sharding import PartitionSpec as P

adapter_scale_factor = 2.0


def contract_last(left, right):
    return lax.dot_general(
        left, right, (((1,), (1,)), ((), ())), preferred_element_type=jnp.float32
    )


def contract_first(left, right):
    return lax.dot_general(
        left, right, (((0,), (0,)), ((), ())), preferred_element_type=jnp.float32
    )


def token_owner(tenant_ids, owner_map):
    tenant_total = owner_map.shape[0]
    match = tenant_ids[:, None] == jnp.arange(tenant_total, dtype=jnp.int32)[None, :]
    return jnp.sum(jnp.where(match, owner_map[None, :], 0), axis=1)


def token_weight(document_index_per_token):
    same_doc = document_index_per_token[:, None] == document_index_per_token[None, :]
    sequence_length = jnp.sum(same_doc.astype(jnp.float32), axis=1)
    return adapter_scale_factor / sequence_length


def after(value, *others):
    return lax.optimization_barrier((value,) + others)[0]


def route_tokens(
    features, cotangent, tenant_ids, document_index_per_token, owner_map, adapter_down, adapter_up
):
    ranks = lax.axis_size("dp")
    rows = features.shape[0]
    width = features.shape[1]
    capacity = max(2, 2 * rows // ranks)
    slots = ranks * capacity
    token_row_index = jnp.arange(rows, dtype=jnp.int32)
    target = token_owner(tenant_ids, owner_map)
    routing_weight = token_weight(document_index_per_token)
    earlier = (token_row_index[:, None] > token_row_index[None, :]) & (
        target[:, None] == target[None, :]
    )
    before = jnp.sum(earlier.astype(jnp.int32), axis=1)
    slot_of = target * capacity + before
    placed = slot_of[None, :] == jnp.arange(slots, dtype=jnp.int32)[:, None]
    slot_weight = jnp.sum(
        jnp.where(placed, routing_weight[None, :], jnp.zeros_like(routing_weight)[None, :]), axis=1
    )

    def pack(values):
        return jnp.dot(
            placed.astype(values.dtype), values, preferred_element_type=jnp.float32
        ).astype(values.dtype)

    def exchange(values):
        return lax.all_to_all(values, "dp", split_axis=0, concat_axis=0, tiled=True)

    down_own = adapter_down[0]
    up_own = adapter_up[0]
    got_x = exchange(pack(features).reshape(ranks, capacity, width)).reshape(slots, width)
    got_g = exchange(pack(cotangent).reshape(ranks, capacity, width)).reshape(slots, width)
    got_w = exchange(slot_weight.reshape(ranks, capacity)).reshape(slots)
    low_h, low_u = lax.psum(
        (contract_last(got_x, down_own), contract_last(got_g, up_own)), "tensor"
    )
    scaled_h = (low_h * got_w[:, None]).astype(jnp.bfloat16)
    scaled_u = (low_u * got_w[:, None]).astype(jnp.bfloat16)
    up_adapter_gradient = contract_first(scaled_h, got_g)
    grad_down = contract_first(scaled_u, got_x)
    slot_dx = jnp.dot(scaled_u, down_own, preferred_element_type=jnp.float32).astype(jnp.bfloat16)
    returned = exchange(slot_dx.reshape(ranks, capacity, width)).reshape(slots, width)
    input_grad = contract_first(placed.astype(jnp.bfloat16), returned).astype(jnp.bfloat16)
    return (input_grad, grad_down[None], up_adapter_gradient[None])


VMEM_LIMIT = 32 * 1024 * 1024


def whole(*shape):
    return pl.BlockSpec(shape, lambda _: (0,) * len(shape))


def column_cut(rows, wide, at):
    return pl.BlockSpec((rows, wide), lambda _: (0, at))


def small_kernel(kernel, out_shape, in_specs, out_specs):
    return pl.pallas_call(
        kernel,
        grid=(1,),
        out_shape=out_shape,
        in_specs=in_specs,
        out_specs=out_specs,
        compiler_params=pltpu.CompilerParams(vmem_limit_bytes=VMEM_LIMIT),
        cost_estimate=pl.CostEstimate(flops=0, bytes_accessed=0, transcendentals=0),
    )


def spread(scaled, held_ref):
    return jnp.concatenate(
        [
            jnp.where(held_ref[step : step + 1, :] > 0, scaled, 0.0).astype(jnp.bfloat16)
            for step in range(held_ref.shape[0])
        ]
    )


def join_kernel(layer_ref, own_ref, *refs):
    *halves, out_ref = refs
    count = len(halves) // 2
    rank = own_ref.shape[0]
    out_ref[:rank, :] = own_ref[...]
    first = layer_ref[0] == 0
    for step in range(count):
        got, other = halves[step][...], halves[count + step][...]
        low = (step + 1) * rank
        middle = low + rank // 2
        out_ref[low:middle, :] = jnp.where(first, got, other)
        out_ref[middle : low + rank, :] = jnp.where(first, other, got)


def join(layer, own, got, other):
    rank, width = own.shape
    rows = (len(got) + 1) * rank
    return small_kernel(
        join_kernel,
        jax.ShapeDtypeStruct((rows, width), own.dtype),
        [pl.BlockSpec(memory_space=pltpu.SMEM), whole(rank, width)]
        + [whole(rank // 2, width)] * (2 * len(got)),
        whole(rows, width),
    )(layer, own, *got, *other)


def project_kernel(adapter_ref, own_ref, other_ref, held_ref, base_ref, out_ref):
    columns, tokens = held_ref.shape
    rows = tokens // 2
    rank = adapter_ref.shape[0] // columns
    adapters = adapter_ref[...]
    for part, rows_ref in enumerate((own_ref, other_ref)):
        cut = slice(part * rows, (part + 1) * rows)
        low = contract_last(adapters, rows_ref[...])
        total = base_ref[:, cut]
        for step in range(columns):
            total = total + jnp.where(
                held_ref[step : step + 1, cut] > 0, low[step * rank : (step + 1) * rank], 0.0
            )
        out_ref[:, cut] = total


def project(adapters, own_rows, other_rows, held, base, at):
    rows, wide = other_rows.shape
    return small_kernel(
        project_kernel,
        jax.ShapeDtypeStruct(base.shape, jnp.float32),
        [
            column_cut(adapters.shape[0], wide, at),
            column_cut(rows, wide, at),
            whole(rows, wide),
            whole(*held.shape),
            whole(*base.shape),
        ],
        whole(*base.shape),
    )(adapters, own_rows, other_rows, held, base)


def partial_kernel(scaled_ref, held_ref, own_ref, other_ref, *out_refs):
    rows = own_ref.shape[0]
    rank = scaled_ref.shape[0]
    left = spread(scaled_ref[...], held_ref)
    wide = out_refs[0].shape[1]
    for i in range(len(out_refs) // 2):
        cut = slice(i * wide, (i + 1) * wide)
        total = jnp.dot(left[:, :rows], own_ref[:, cut], preferred_element_type=jnp.float32)
        total = total + jnp.dot(
            left[:, rows:], other_ref[:, cut], preferred_element_type=jnp.float32
        )
        for out_ref, blocks in zip(out_refs[2 * i : 2 * i + 2], ((0, 2), (1, 3))):
            for at, block in enumerate(blocks):
                out_ref[at * rank : (at + 1) * rank, :] = total[
                    block * rank : (block + 1) * rank
                ].astype(out_ref.dtype)


def partials(scaled, held, own_rows, other_rows, at, pieces):
    rows, wide = other_rows.shape
    shape = (2 * scaled.shape[0], wide // pieces)
    kinds = [jnp.float32, jnp.bfloat16] * pieces
    return small_kernel(
        partial_kernel,
        [jax.ShapeDtypeStruct(shape, kind) for kind in kinds],
        [
            whole(*scaled.shape),
            whole(*held.shape),
            column_cut(rows, wide, at),
            whole(rows, wide),
        ],
        [whole(*shape)] * len(kinds),
    )(scaled, held, own_rows, other_rows)


def add_kernel(*refs):
    *parts, out_ref = refs
    rank = out_ref.shape[1]
    wide = parts[0].shape[1]
    for i in range(len(parts) // 3):
        total = parts[3 * i][:rank, :]
        for part in parts[3 * i + 1 : 3 * i + 3]:
            total = total + part[:rank, :].astype(jnp.float32)
        out_ref[0, :, i * wide : (i + 1) * wide] = total


def add_parts(groups, rank, width):
    operands = [part for group in groups for part in group]
    return small_kernel(
        add_kernel,
        jax.ShapeDtypeStruct((1, rank, width), jnp.float32),
        [whole(*operand.shape) for operand in operands],
        whole(1, rank, width),
    )(*operands)


def input_grad_kernel(low_ref, low_there_ref, held_ref, held_there_ref, down_ref, there_ref, dx_ref):
    dx = contract_first(spread(low_ref[...], held_ref), down_ref[...])
    dx = dx + contract_first(spread(low_there_ref[...], held_there_ref), there_ref[...])
    dx_ref[...] = dx.astype(dx_ref.dtype)


def input_gradient(*operands):
    shape = (operands[0].shape[1], operands[-1].shape[1])
    return small_kernel(
        input_grad_kernel,
        jax.ShapeDtypeStruct(shape, jnp.bfloat16),
        [whole(*operand.shape) for operand in operands],
        whole(*shape),
    )(*operands)


def route_adapters(
    features, cotangent, tenant_ids, document_index_per_token, owner_map, adapter_down, adapter_up
):
    ranks = lax.axis_size("dp")
    columns = ranks // 2
    rows, width = features.shape
    rank = adapter_down.shape[1]
    half = rank // 2
    me = lax.axis_index("dp")
    side, place = me % 2, me // 2
    layer = lax.axis_index("parts")

    def swap_side(value):
        return lax.ppermute(value, "dp", [(i, i ^ 1) for i in range(ranks)])

    def hop(value, by):
        return lax.ppermute(value, "dp", [(i, i ^ (2 * by)) for i in range(ranks)])

    def swap_layer(value):
        return lax.ppermute(value, "parts", [(0, 1), (1, 0)])

    def swap_core(value):
        return lax.ppermute(value, "tensor", [(0, 1), (1, 0)])

    def fetch(own):
        mine = lax.dynamic_slice(own, (layer * half, 0), (half, width))
        got = {step: hop(mine, step) for step in range(columns - 1, 0, -1)}
        return [got[step] for step in range(1, columns)]

    pieces = 2
    wide = width // pieces
    layer_of = layer.astype(jnp.int32)[None]
    other_x = swap_side(features)
    ids_there = swap_side(jnp.stack([tenant_ids, document_index_per_token]))
    down_own = after(adapter_down[0], ids_there)
    own_g = [cotangent[:, i * wide : (i + 1) * wide] for i in range(pieces)]
    down_got = fetch(down_own)
    down = join(layer_of, down_own, down_got, [swap_layer(got) for got in down_got])
    up_own = after(adapter_up[0], down_got[0])
    up_got = fetch(up_own)
    up_halves = up_got
    up = join(layer_of, up_own, up_halves, [swap_layer(got) for got in up_halves])
    ids_there = after(ids_there, down)
    other_g = [swap_side(cut) for cut in own_g]

    owner, owner_there = token_owner(tenant_ids, owner_map), token_owner(ids_there[0], owner_map)
    weight = token_weight(document_index_per_token)
    owner_here = jnp.concatenate([owner, owner_there])
    weight_here = jnp.concatenate([weight, token_weight(ids_there[1])])
    block_owner = (place ^ jnp.arange(columns, dtype=jnp.int32)) * 2 + side
    block_owner_there = block_owner + 1 - 2 * side
    held = (block_owner[:, None] == owner_here[None, :]).astype(jnp.float32)
    own_held = (block_owner[:, None] == owner[None, :]).astype(jnp.float32)
    own_there = (block_owner_there[:, None] == owner[None, :]).astype(jnp.float32)

    def combine(low):
        return ((low + swap_core(low)) * weight_here[None, :]).astype(jnp.bfloat16)

    def second_block(kept, came):
        return (kept[rank:] + came[rank:].astype(jnp.float32)).astype(jnp.bfloat16)

    nothing = jnp.zeros((rank, 2 * rows), jnp.float32)
    x_in = after(other_x, *up_got)
    scaled_h = combine(project(down, features, x_in, held, nothing, 0))

    first_g = after(other_g[0], up)
    kept, away = partials(scaled_h, held, cotangent, first_g, 0, 1)
    came = hop(away, 1)
    onward = second_block(kept, came)
    up_groups = [(kept, came, hop(onward, 2))]
    low_u = project(up, cotangent, after(first_g, kept), held, nothing, 0)
    low_u = project(up, cotangent, other_g[1], held, low_u, 1)
    scaled_u = after(combine(low_u), onward)

    outs = partials(scaled_u, held, features, other_x, 0, pieces)
    down_kept, down_came = outs[0::2], [hop(away, 1) for away in outs[1::2]]
    kept, away = partials(scaled_h, held, cotangent, after(other_g[1], outs[0]), 1, 1)
    came = hop(away, 1)
    down_groups = [
        (kept_x, came_x, hop(second_block(kept_x, came_x), 2))
        for kept_x, came_x in zip(down_kept, down_came)
    ]
    onward = second_block(kept, after(came, outs[0]))
    up_groups.append((kept, came, hop(onward, 2)))
    back = swap_side(after(scaled_u, down_came[0])[:, rows:])
    down_there = swap_side(down)
    up_adapter_gradient = add_parts(up_groups, rank, width)
    input_grad = input_gradient(scaled_u[:, :rows], back, own_held, own_there, down, down_there)
    kept, came, last = down_groups[-1]
    down_groups[-1] = (kept, came, after(last, input_grad))
    grad_down = add_parts(down_groups, rank, width)
    return (input_grad, grad_down, up_adapter_gradient)


def shards(features, *others):
    ranks = lax.axis_size("dp")
    rank = others[-1].shape[1]
    slots = 2 * features.shape[0] // ranks
    fits = rank % 32 == 0 and features.shape[1] % 1024 == 0
    if slots >= rank and fits and ranks == 8 and lax.axis_size("parts") == 2:
        return route_adapters(features, *others)
    return route_tokens(features, *others)


def solution(mesh):
    return jax.shard_map(
        shards,
        mesh=mesh,
        in_specs=(
            P(("parts", "dp"), "tensor"),
            P(("parts", "dp"), "tensor"),
            P(("parts", "dp")),
            P(("parts", "dp")),
            P(),
            P("dp", None, "tensor"),
            P("dp", None, "tensor"),
        ),
        out_specs=(
            P(("parts", "dp"), "tensor"),
            P(("parts", "dp"), None, "tensor"),
            P(("parts", "dp"), None, "tensor"),
        ),
        check_vma=False,
    )
```
